32 devices in a mesh: groups: 2 (over y), wide: 4 (over z), layer: 2 (over core), mp: 2 (over x).
Axes of the slice: x: 2, y: 2, z: 4, core: 2. Of those that a mesh axis runs over, the one named last changes fastest.
Arguments:
- acts: bfloat16 [2, 16384, 4096], P('layer', ('groups', 'wide'), 'mp'), parts along dimension 1, may hold values from -6 to 6
- grads: bfloat16 [2, 16384, 4096], P('layer', ('groups', 'wide'), 'mp'), parts along dimension 1, may hold values from -6 to 6
- projections: bfloat16 [2, 4096, 128], P('layer', 'mp'), may hold values from -0.09375 to 0.09375
- lengths: int32 [64], P(('groups', 'wide')), parts along dimension 0, may hold values from 1 to 256, as said below
- queries: bfloat16 [2, 1024, 4096], P('layer', ('groups', 'wide'), 'mp'), parts along dimension 1, may hold values from -0.0625 to 0.0625
- query_ids: int32 [1024], P(('groups', 'wide')), parts along dimension 0, may hold values from 0 to 511, each once
Outputs:
- scores: float32 [64, 512], P(('groups', 'wide')), parts along dimension 0
The draws below stay inside these ranges and needn't reach their ends.
There are 2 independent parts, one for each index of `groups`. The reference program is written for one: setup_inputs(seed, part) draws one part's arguments, and reference() takes and returns one part's arrays. A program takes and returns all parts, laid end to end along the dimension named above; an argument that names none is the same for every part. Nothing has to cross between parts.
Inputs may be any that keep to these rules, and one draw needn't show every extreme that they name: The lengths of one index of wide's 8 examples sum to at most 2048, and to exactly 2048 on at least one index.
All inputs are finite; a program needn't handle non-finite values.
Results may differ from the reference program's by a relative error of at most 0.0029.
Values may be sent and summed in bfloat16 or wider, within the bound.
A program may use at most 64 MiB of HBM per device.

```python
import jax
import jax.numpy as jnp
from jax import lax

D = 4096
R = 64
TOK_DEV = 2048
EX_DEV = 8
LAYERS = 2
TOKENS = 8192
EXAMPLES = 32
QUERIES = 512
N_WIDE = 4


def draw_lengths(key, part):
    key = jax.random.fold_in(key, 11)
    key_one, key_two = jax.random.split(key, 2)
    longest = TOK_DEV // EX_DEV
    base = jax.random.randint(key_one, (N_WIDE, EX_DEV), 1, longest + 1)
    filled = jax.random.randint(key_two, (), 0, N_WIDE)
    blocks = jnp.arange(N_WIDE)[:, None]
    columns = jnp.arange(EX_DEV)[None, :]
    base = jnp.where(blocks == filled, longest, base)
    shortest = (filled + 1) % N_WIDE
    base = jnp.where((blocks == shortest) & (columns == 0), 1, base)
    return base.reshape(-1).astype(jnp.int32)


def shard_levels(own_key, shape, shards, least, largest):
    def one(dim, parts):
        heights = jax.random.uniform(jax.random.fold_in(jax.random.fold_in(own_key, 6), dim), (parts,), jnp.float32, least / len(shards), largest / len(shards))
        return jnp.repeat(jnp.exp(heights), shape[dim] // parts).reshape((-1,) + (1,) * (len(shape) - dim - 1))

    level = one(*shards[0])
    for cut in shards[1:]:
        level = level * one(*cut)
    return level


def centred(key, extent, deviation, bound, pieces=(), kind=jnp.bfloat16):
    factor_of = shard_levels(key, extent, pieces, -0.22, 0.18) if pieces else 1.0
    array = jax.random.normal(key, extent, jnp.float32) * deviation * factor_of
    return jnp.minimum(jnp.maximum(array, -bound), bound).astype(kind)


def setup_inputs(seed: int = 0, part: int = 0) -> dict:
    key_list = jax.random.split(jax.random.key(seed), 7)
    own_keys = jax.random.split(jax.random.fold_in(key_list[6], part), 7)
    acts = centred(own_keys[0], (LAYERS, TOKENS, D), 1.0, 6.0, ((0, 2), (1, 4), (2, 2)))
    grads = centred(own_keys[1], (LAYERS, TOKENS, D), 1.0, 6.0, ((0, 2), (1, 4), (2, 2)))
    projections = centred(key_list[2], (LAYERS, D, 2 * R), D ** -0.5, 0.09375, ((0, 2), (1, 2)))
    lengths = draw_lengths(jax.random.fold_in(jax.random.fold_in(key_list[6], part), 71), part)
    queries = centred(own_keys[4], (LAYERS, QUERIES, R * R), (LAYERS * R * R) ** -0.5, 0.0625, ((0, 2), (1, 4), (2, 2)))
    query_ids = jax.random.permutation(own_keys[5], QUERIES).astype(jnp.int32)
    return {"acts": acts, "grads": grads, "projections": projections, "lengths": lengths, "queries": queries, "query_ids": query_ids}


def block_sketch(packed):
    proj_x, proj_g, lens = packed
    ends = jnp.cumsum(lens)
    starts = ends - lens
    rows = jnp.arange(TOK_DEV, dtype=jnp.int32)
    member = ((rows[None, :] >= starts[:, None]) & (rows[None, :] < ends[:, None])).astype(jnp.float32)
    weighted = member[:, None, :] * jnp.transpose(proj_g)[None, :, :]
    sums = jnp.einsum('eat,tb->eab', weighted, proj_x, precision=lax.Precision.HIGHEST)
    sums = sums / jnp.sqrt(lens.astype(jnp.float32))[:, None, None]
    return sums.reshape(EX_DEV, R * R)

def reference(acts, grads, projections, lengths, queries, query_ids):
    total = jnp.zeros((EXAMPLES, QUERIES), jnp.float32)
    lens = lengths.reshape(N_WIDE, EX_DEV)
    for level in range(LAYERS):
        proj_x = jnp.dot(acts[level], projections[level][:, :R], preferred_element_type=jnp.float32)
        proj_g = jnp.dot(grads[level], projections[level][:, R:], preferred_element_type=jnp.float32)
        sketch = lax.map(block_sketch, (proj_x.reshape(N_WIDE, TOK_DEV, R), proj_g.reshape(N_WIDE, TOK_DEV, R), lens))
        sketch = sketch.reshape(EXAMPLES, R * R).astype(jnp.bfloat16)
        total = total + jnp.dot(sketch, jnp.transpose(queries[level]), preferred_element_type=jnp.float32)
    scores = jnp.zeros((EXAMPLES, QUERIES), jnp.float32).at[:, query_ids].set(total)
    return scores
```

```python
import functools

import jax
import jax.numpy as jnp
from jax import lax
from jax.experimental import pallas as pl
from jax.experimental.pallas import tpu as pltpu
from jax.sharding import PartitionSpec as P

MESH = pl.DeviceIdType.MESH
F32 = jnp.float32
BF16 = jnp.bfloat16
NT = (((1,), (1,)), ((), ()))


def each(first, last, body):
    if last - first <= 16:
        for i in range(first, last):
            body(i)
    else:
        pl.loop(first, last)(body)


def kernel(
    sizes, acts, grads, proj, lens, queries, ids, out,
    a_buf, g_buf, w_buf, wx_buf, q_buf, id_buf, len_buf,
    g_own, g_send, g_recv, acc, part, part_recv, s_send, s_recv,
    sc_send, sc_recv, onehot,
    in_sem, a_sem, gr_sem, g_ssem, g_rsem, p_ssem, p_rsem,
    s_ssem, s_rsem, id_ssem, id_rsem, sc_ssem, sc_rsem,
):
    W, L, M = sizes
    N = W * L * M
    w = lax.axis_index("wide")
    l = lax.axis_index("layer")
    m = lax.axis_index("mp")
    me = (w * L + l) * M + m
    n_chunk, C, _ = a_buf.shape
    rank = w_buf.shape[1] // 2
    ex = len_buf.shape[0]
    mine_pairs = part_recv.shape[1]

    def local(src, dst, sem):
        return pltpu.make_async_copy(src, dst, sem)

    def rows(c):
        return pl.ds(pl.multiple_of(c * C, C), C)

    local(proj.at[0], w_buf, in_sem.at[0]).start()
    local(lens, len_buf, in_sem.at[1]).start()
    for c in range(n_chunk):
        local(grads.at[0, rows(c)], g_buf.at[c], gr_sem.at[c]).start()
    for c in range(n_chunk):
        local(acts.at[0, rows(c)], a_buf.at[c], a_sem.at[c]).start()
    local(ids, id_buf.at[w], in_sem.at[2]).start()
    local(queries.at[0], q_buf, in_sem.at[3]).start()

    barrier = pltpu.get_barrier_semaphore()

    def place(d):
        other = lax.rem(me + d, N)
        return other // (L * M), (other // M) % L, other % M

    def greet(d):
        ow, ol, om = place(d)
        pl.semaphore_signal(
            barrier, inc=1, device_id={"wide": ow, "layer": ol, "mp": om}, device_id_type=MESH
        )

    each(1, N, greet)

    sub = lax.broadcasted_iota(jnp.int32, (ex, C), 0)
    lane = lax.broadcasted_iota(jnp.int32, (ex, C), 1)
    local(lens, len_buf, in_sem.at[1]).wait()
    first = jnp.zeros((ex, C), jnp.int32)
    last = jnp.zeros((ex, C), jnp.int32)
    run = jnp.int32(0)
    for e in range(ex):
        first = jnp.where(sub == e, run, first)
        run = run + len_buf[e]
        last = jnp.where(sub == e, run, last)

    acc[...] = jnp.zeros_like(acc)
    local(proj.at[0], w_buf, in_sem.at[0]).wait()
    wx = w_buf[:, :rank]
    wx_buf[...] = jnp.concatenate([wx, wx], axis=1)

    def g_copy(d, c):
        to = lax.rem(m + d, M)
        return pltpu.make_async_remote_copy(
            src_ref=g_send.at[c],
            dst_ref=g_recv.at[d - 1, c],
            send_sem=g_ssem.at[d - 1, c],
            recv_sem=g_rsem.at[d - 1, c],
            device_id={"mp": to},
            device_id_type=MESH,
        )

    def project_g(c):
        local(grads.at[0, rows(c)], g_buf.at[c], gr_sem.at[c]).wait()
        g = jnp.dot(g_buf[c], w_buf[...], preferred_element_type=F32)
        gt = jnp.transpose(g)[rank:, :]
        g_own[c] = gt
        g_send[c] = gt.astype(BF16)

    project_g(0)
    pl.semaphore_wait(barrier, N - 1)
    for d in range(1, M):
        g_copy(d, 0).start()

    @pl.loop(1, n_chunk)
    def _(c):
        project_g(c)
        for d in range(1, M):
            g_copy(d, c).start()

    local(ids, id_buf.at[w], in_sem.at[2]).wait()

    def id_copy(d):
        return pltpu.make_async_remote_copy(
            src_ref=id_buf.at[w],
            dst_ref=id_buf.at[w],
            send_sem=id_ssem.at[d - 1],
            recv_sem=id_rsem.at[d - 1],
            device_id={"wide": lax.rem(w + d, W)},
            device_id_type=MESH,
        )

    for d in range(1, W):
        id_copy(d).start()

    @pl.loop(0, n_chunk)
    def _(c):
        local(acts.at[0, rows(c)], a_buf.at[c], a_sem.at[c]).wait()
        x = jnp.dot(a_buf[c], wx_buf[...], preferred_element_type=F32)
        x_hi = x.astype(BF16)
        x_lo = (x - x_hi.astype(F32)).astype(BF16)
        right = jnp.concatenate([x_hi, x_lo], axis=1)
        g = g_own[c]
        for d in range(1, M):
            g_copy(d, c).wait_recv()
            g = g + g_recv[d - 1, c].astype(F32)
        g_hi = g.astype(BF16).astype(F32)
        g_lo = g - g_hi
        t = lane + c * C
        member = (t >= first) & (t < last)
        for i, side in enumerate((g_hi, g_lo)):
            left = jnp.concatenate(
                [
                    jnp.where(member, jnp.broadcast_to(side[a : a + 1, :], (ex, C)), 0.0)
                    for a in range(rank)
                ],
                axis=0,
            ).astype(BF16)
            acc[i] += jnp.dot(left, right, preferred_element_type=F32)

    wide_lane = lax.broadcasted_iota(jnp.int32, (rank // 2, ex, 2 * rank), 2)
    sums = acc[0, :, : 2 * rank] + acc[0, :, 2 * rank :] + acc[1, :, : 2 * rank]
    sums = sums.reshape(rank // 2, 2, ex, 2 * rank)
    part[...] = jnp.where(wide_lane < rank, sums[:, 0], sums[:, 1])

    def p_copy(d):
        to = lax.rem(m + d, M)
        return pltpu.make_async_remote_copy(
            src_ref=part.at[pl.ds(to * mine_pairs, mine_pairs)],
            dst_ref=part_recv.at[d - 1],
            send_sem=p_ssem.at[d - 1],
            recv_sem=p_rsem.at[d - 1],
            device_id={"mp": to},
            device_id_type=MESH,
        )

    for d in range(1, M):
        p_copy(d).start()

    root = jnp.zeros((ex, 2 * rank), jnp.int32)
    for e in range(ex):
        root = jnp.where(sub[:, : 2 * rank] == e, len_buf[e], root)
    root = jnp.sqrt(root.astype(F32))

    for d in range(1, W):
        id_copy(d).wait()
    q_rows = id_buf.shape[2]
    for v in range(W):
        number = lax.broadcasted_iota(jnp.int32, (W * q_rows, q_rows), 0)
        onehot[:, v * q_rows : (v + 1) * q_rows] = jnp.where(
            number == id_buf[v], 1.0, 0.0
        ).astype(BF16)
    local(queries.at[0], q_buf, in_sem.at[3]).wait()

    total = part[pl.ds(m * mine_pairs, mine_pairs)]
    for d in range(1, M):
        p_copy(d).wait_recv()
        total = total + part_recv[d - 1]
    sketch = total / root[None]
    s_send[...] = sketch.reshape(mine_pairs * ex, 2 * rank).astype(BF16)

    def s_copy(d):
        return pltpu.make_async_remote_copy(
            src_ref=s_send,
            dst_ref=s_recv.at[d - 1],
            send_sem=s_ssem.at[d - 1],
            recv_sem=s_rsem.at[d - 1],
            device_id={"wide": lax.rem(w + d, W)},
            device_id_type=MESH,
        )

    for d in range(1, W):
        s_copy(d).start()

    def score(block):
        block = block.astype(F32).reshape(mine_pairs, ex, 2 * rank)
        left = jnp.concatenate([block[k] for k in range(mine_pairs)], axis=1).astype(BF16)
        return lax.dot_general(left, q_buf[...], NT, preferred_element_type=F32)

    def sc_copy(ow, lm):
        other = lax.rem(l * M + m + lm, L * M)
        slot = (lax.rem(ow - w + W, W)) * (L * M) + lm
        return pltpu.make_async_remote_copy(
            src_ref=sc_send.at[ow],
            dst_ref=sc_recv.at[w, lm],
            send_sem=sc_ssem.at[slot],
            recv_sem=sc_rsem.at[w, lm],
            device_id={"wide": ow, "layer": other // M, "mp": other % M},
            device_id_type=MESH,
        )

    own = score(s_send[...])
    sc_send[w] = own
    for lm in range(1, L * M):
        sc_copy(w, lm).start()
    for d in range(1, W):
        s_copy(d).wait_recv()
        ow = lax.rem(w - d + W, W)
        sc_send[ow] = score(s_recv[d - 1])
        for lm in range(L * M):
            sc_copy(ow, lm).start()

    sc_recv[w, 0] = own

    def arrive(v, lm):
        sc = sc_recv.at[v, lm]
        pltpu.make_async_copy(sc, sc, sc_rsem.at[v, lm]).wait()

    for lm in range(1, L * M):
        arrive(w, lm)
    for d in range(1, W):
        v = lax.rem(w + d, W)
        for lm in range(L * M):
            arrive(v, lm)
    blocks = []
    for v in range(W):
        block = sc_recv[v, 0]
        for lm in range(1, L * M):
            block = block + sc_recv[v, lm]
        blocks.append(block)
    scores = jnp.concatenate(blocks, axis=1)
    high = scores.astype(BF16).astype(F32)
    rest = scores - high
    middle = rest.astype(BF16).astype(F32)
    low = rest - middle
    pieces = jnp.concatenate([high, middle, low, jnp.zeros_like(low)], axis=0).astype(BF16)
    placed = lax.dot_general(pieces, onehot[...], NT, preferred_element_type=F32)
    out[...] = placed[:ex] + placed[ex : 2 * ex] + placed[2 * ex : 3 * ex]

    for d in range(1, M):
        p_copy(d).wait_send()
        for c in range(n_chunk):
            g_copy(d, c).wait_send()
    for d in range(1, W):
        s_copy(d).wait_send()
    for d in range(W):
        ow = lax.rem(w - d + W, W)
        for lm in range(1 if d == 0 else 0, L * M):
            sc_copy(ow, lm).wait_send()


def per_device(acts, grads, projections, lengths, queries, query_ids):
    W, L, M = (lax.axis_size(name) for name in ("wide", "layer", "mp"))
    _, tokens, depth = acts.shape
    rank2 = projections.shape[2]
    rank = rank2 // 2
    ex = lengths.shape[0]
    q_rows = queries.shape[1]
    C = 256
    n_chunk = tokens // C
    mine_pairs = rank // 2 // M
    dma = pltpu.SemaphoreType.DMA
    moves = tokens * depth * 4 + depth * rank2 * 2 + q_rows * depth * 2
    return pl.pallas_call(
        functools.partial(kernel, (W, L, M)),
        out_shape=jax.ShapeDtypeStruct((ex, q_rows * W), F32),
        in_specs=[pl.BlockSpec(memory_space=pl.ANY)] * 6,
        out_specs=pl.BlockSpec(memory_space=pltpu.VMEM),
        scratch_shapes=[
            pltpu.VMEM((n_chunk, C, depth), BF16),
            pltpu.VMEM((n_chunk, C, depth), BF16),
            pltpu.VMEM((depth, rank2), BF16),
            pltpu.VMEM((depth, rank2), BF16),
            pltpu.VMEM((q_rows, depth), BF16),
            pltpu.VMEM((W, 1, q_rows), jnp.int32),
            pltpu.SMEM((ex,), jnp.int32),
            pltpu.VMEM((n_chunk, rank, C), F32),
            pltpu.VMEM((n_chunk, rank, C), BF16),
            pltpu.VMEM((max(M - 1, 1), n_chunk, rank, C), BF16),
            pltpu.VMEM((2, rank * ex, 2 * rank2), F32),
            pltpu.VMEM((rank // 2, ex, rank2), F32),
            pltpu.VMEM((max(M - 1, 1), mine_pairs, ex, rank2), F32),
            pltpu.VMEM((mine_pairs * ex, rank2), BF16),
            pltpu.VMEM((max(W - 1, 1), mine_pairs * ex, rank2), BF16),
            pltpu.VMEM((W, ex, q_rows), F32),
            pltpu.VMEM((W, L * M, ex, q_rows), F32),
            pltpu.VMEM((q_rows * W, q_rows * W), BF16),
            dma((4,)),
            dma((n_chunk,)),
            dma((n_chunk,)),
            dma((max(M - 1, 1), n_chunk)),
            dma((max(M - 1, 1), n_chunk)),
            dma((max(M - 1, 1),)),
            dma((max(M - 1, 1),)),
            dma((max(W - 1, 1),)),
            dma((max(W - 1, 1),)),
            dma((max(W - 1, 1),)),
            dma((max(W - 1, 1),)),
            dma((W * L * M,)),
            dma((W, L * M)),
        ],
        compiler_params=pltpu.CompilerParams(
            collective_id=0, has_side_effects=True, vmem_limit_bytes=56 * 1024 * 1024
        ),
        cost_estimate=pl.CostEstimate(
            flops=tokens * depth * rank2 * 4, bytes_accessed=moves, transcendentals=0
        ),
    )(acts, grads, projections, lengths, queries, query_ids.reshape(1, q_rows))


def solution(mesh):
    return jax.shard_map(
        per_device,
        mesh=mesh,
        in_specs=(
            P("layer", ("groups", "wide"), "mp"),
            P("layer", ("groups", "wide"), "mp"),
            P("layer", "mp", None),
            P(("groups", "wide")),
            P("layer", ("groups", "wide"), "mp"),
            P(("groups", "wide")),
        ),
        out_specs=P(("groups", "wide"), None),
        check_vma=False,
    )
```

```python
import functools

import jax
import jax.numpy as jnp
from jax import lax
from jax.experimental import pallas as pl
from jax.experimental.pallas import tpu as pltpu
from jax.sharding import PartitionSpec as P

MESH = pl.DeviceIdType.MESH
F32 = jnp.float32
BF16 = jnp.bfloat16
NT = (((1,), (1,)), ((), ()))


def each(first, last, body):
    if last - first <= 16:
        for i in range(first, last):
            body(i)
    else:
        pl.loop(first, last)(body)


def kernel(
    sizes, acts, grads, proj, lens, queries, ids, out,
    a_buf, g_buf, w_buf, wx_buf, q_buf, id_buf, len_buf,
    g_own, g_send, g_recv, acc, part, part_recv, s_send, s_recv,
    sc_send, sc_recv, onehot,
    in_sem, a_sem, gr_sem, g_ssem, g_rsem, p_ssem, p_rsem,
    s_ssem, s_rsem, id_ssem, id_rsem, sc_ssem, sc_rsem,
):
    W, L, M = sizes
    N = W * L * M
    w = lax.axis_index("wide")
    l = lax.axis_index("layer")
    m = lax.axis_index("mp")
    me = (w * L + l) * M + m
    n_chunk, C, _ = a_buf.shape
    rank = w_buf.shape[1] // 2
    ex = len_buf.shape[0]
    mine_pairs = part_recv.shape[1]

    def local(src, dst, sem):
        return pltpu.make_async_copy(src, dst, sem)

    def rows(c):
        return pl.ds(pl.multiple_of(c * C, C), C)

    local(proj.at[0], w_buf, in_sem.at[0]).start()
    local(lens, len_buf, in_sem.at[1]).start()
    for c in range(n_chunk):
        local(grads.at[0, rows(c)], g_buf.at[c], gr_sem.at[c]).start()
    for c in range(n_chunk):
        local(acts.at[0, rows(c)], a_buf.at[c], a_sem.at[c]).start()
    local(ids, id_buf.at[w], in_sem.at[2]).start()
    local(queries.at[0], q_buf, in_sem.at[3]).start()

    barrier = pltpu.get_barrier_semaphore()

    def place(d):
        other = lax.rem(me + d, N)
        return other // (L * M), (other // M) % L, other % M

    def greet(d):
        ow, ol, om = place(d)
        pl.semaphore_signal(
            barrier, inc=1, device_id={"wide": ow, "layer": ol, "mp": om}, device_id_type=MESH
        )

    each(1, N, greet)

    sub = lax.broadcasted_iota(jnp.int32, (ex, C), 0)
    lane = lax.broadcasted_iota(jnp.int32, (ex, C), 1)
    local(lens, len_buf, in_sem.at[1]).wait()
    first = jnp.zeros((ex, C), jnp.int32)
    last = jnp.zeros((ex, C), jnp.int32)
    run = jnp.int32(0)
    for e in range(ex):
        first = jnp.where(sub == e, run, first)
        run = run + len_buf[e]
        last = jnp.where(sub == e, run, last)

    acc[...] = jnp.zeros_like(acc)
    local(proj.at[0], w_buf, in_sem.at[0]).wait()
    wx = w_buf[:, :rank]
    wx_buf[...] = jnp.concatenate([wx, wx], axis=1)

    def g_copy(d, c):
        to = lax.rem(m + d, M)
        return pltpu.make_async_remote_copy(
            src_ref=g_send.at[c],
            dst_ref=g_recv.at[d - 1, c],
            send_sem=g_ssem.at[d - 1, c],
            recv_sem=g_rsem.at[d - 1, c],
            device_id={"mp": to},
            device_id_type=MESH,
        )

    def project_g(c):
        local(grads.at[0, rows(c)], g_buf.at[c], gr_sem.at[c]).wait()
        g = jnp.dot(g_buf[c], w_buf[...], preferred_element_type=F32)
        gt = jnp.transpose(g)[rank:, :]
        g_own[c] = gt
        g_send[c] = gt.astype(BF16)

    project_g(0)
    pl.semaphore_wait(barrier, N - 1)
    for d in range(1, M):
        g_copy(d, 0).start()

    @pl.loop(1, n_chunk)
    def _(c):
        project_g(c)
        for d in range(1, M):
            g_copy(d, c).start()

    local(ids, id_buf.at[w], in_sem.at[2]).wait()

    def id_copy(d):
        return pltpu.make_async_remote_copy(
            src_ref=id_buf.at[w],
            dst_ref=id_buf.at[w],
            send_sem=id_ssem.at[d - 1],
            recv_sem=id_rsem.at[d - 1],
            device_id={"wide": lax.rem(w + d, W)},
            device_id_type=MESH,
        )

    for d in range(1, W):
        id_copy(d).start()

    @pl.loop(0, n_chunk)
    def _(c):
        local(acts.at[0, rows(c)], a_buf.at[c], a_sem.at[c]).wait()
        x = jnp.dot(a_buf[c], wx_buf[...], preferred_element_type=F32)
        x_hi = x.astype(BF16)
        x_lo = (x - x_hi.astype(F32)).astype(BF16)
        right = jnp.concatenate([x_hi, x_lo], axis=1)
        g = g_own[c]
        for d in range(1, M):
            g_copy(d, c).wait_recv()
            g = g + g_recv[d - 1, c].astype(F32)
        g_hi = g.astype(BF16).astype(F32)
        g_lo = g - g_hi
        t = lane + c * C
        member = (t >= first) & (t < last)
        for i, side in enumerate((g_hi, g_lo)):
            left = jnp.concatenate(
                [
                    jnp.where(member, jnp.broadcast_to(side[a : a + 1, :], (ex, C)), 0.0)
                    for a in range(rank)
                ],
                axis=0,
            ).astype(BF16)
            acc[i] += jnp.dot(left, right, preferred_element_type=F32)

    wide_lane = lax.broadcasted_iota(jnp.int32, (rank // 2, ex, 2 * rank), 2)
    sums = acc[0, :, : 2 * rank] + acc[0, :, 2 * rank :] + acc[1, :, : 2 * rank]
    sums = sums.reshape(rank // 2, 2, ex, 2 * rank)
    part[...] = jnp.where(wide_lane < rank, sums[:, 0], sums[:, 1])

    def p_copy(d):
        to = lax.rem(m + d, M)
        return pltpu.make_async_remote_copy(
            src_ref=part.at[pl.ds(to * mine_pairs, mine_pairs)],
            dst_ref=part_recv.at[d - 1],
            send_sem=p_ssem.at[d - 1],
            recv_sem=p_rsem.at[d - 1],
            device_id={"mp": to},
            device_id_type=MESH,
        )

    for d in range(1, M):
        p_copy(d).start()

    root = jnp.zeros((ex, 2 * rank), jnp.int32)
    for e in range(ex):
        root = jnp.where(sub[:, : 2 * rank] == e, len_buf[e], root)
    root = jnp.sqrt(root.astype(F32))

    for d in range(1, W):
        id_copy(d).wait()
    q_rows = id_buf.shape[2]
    for v in range(W):
        number = lax.broadcasted_iota(jnp.int32, (W * q_rows, q_rows), 0)
        onehot[:, v * q_rows : (v + 1) * q_rows] = jnp.where(
            number == id_buf[v], 1.0, 0.0
        ).astype(BF16)
    local(queries.at[0], q_buf, in_sem.at[3]).wait()

    total = part[pl.ds(m * mine_pairs, mine_pairs)]
    for d in range(1, M):
        p_copy(d).wait_recv()
        total = total + part_recv[d - 1]
    sketch = total / root[None]
    s_send[...] = sketch.reshape(mine_pairs * ex, 2 * rank).astype(BF16)

    def s_copy(d):
        return pltpu.make_async_remote_copy(
            src_ref=s_send,
            dst_ref=s_recv.at[d - 1],
            send_sem=s_ssem.at[d - 1],
            recv_sem=s_rsem.at[d - 1],
            device_id={"wide": lax.rem(w + d, W)},
            device_id_type=MESH,
        )

    for d in range(1, W):
        s_copy(d).start()

    def score(block):
        block = block.astype(F32).reshape(mine_pairs, ex, 2 * rank)
        left = jnp.concatenate([block[k] for k in range(mine_pairs)], axis=1).astype(BF16)
        return lax.dot_general(left, q_buf[...], NT, preferred_element_type=F32)

    def sc_copy(ow, lm):
        other = lax.rem(l * M + m + lm, L * M)
        slot = (lax.rem(ow - w + W, W)) * (L * M) + lm
        return pltpu.make_async_remote_copy(
            src_ref=sc_send.at[ow],
            dst_ref=sc_recv.at[w, lm],
            send_sem=sc_ssem.at[slot],
            recv_sem=sc_rsem.at[w, lm],
            device_id={"wide": ow, "layer": other // M, "mp": other % M},
            device_id_type=MESH,
        )

    own = score(s_send[...])
    sc_send[w] = own
    for lm in range(1, L * M):
        sc_copy(w, lm).start()
    for d in range(1, W):
        s_copy(d).wait_recv()
        ow = lax.rem(w - d + W, W)
        sc_send[ow] = score(s_recv[d - 1])
        for lm in range(L * M):
            sc_copy(ow, lm).start()

    sc_recv[w, 0] = own

    def arrive(v, lm):
        sc = sc_recv.at[v, lm]
        pltpu.make_async_copy(sc, sc, sc_rsem.at[v, lm]).wait()

    for lm in range(1, L * M):
        arrive(w, lm)
    for d in range(1, W):
        v = lax.rem(w + d, W)
        for lm in range(L * M):
            arrive(v, lm)
    blocks = []
    for v in range(W):
        block = sc_recv[v, 0]
        for lm in range(1, L * M):
            block = block + sc_recv[v, lm]
        blocks.append(block)
    scores = jnp.concatenate(blocks, axis=1)
    high = scores.astype(BF16).astype(F32)
    rest = scores - high
    middle = rest.astype(BF16).astype(F32)
    low = rest - middle
    pieces = jnp.concatenate([high, middle, low, jnp.zeros_like(low)], axis=0).astype(BF16)
    placed = lax.dot_general(pieces, onehot[...], NT, preferred_element_type=F32)
    out[...] = placed[:ex] + placed[ex : 2 * ex] + placed[2 * ex : 3 * ex]

    for d in range(1, M):
        p_copy(d).wait_send()
        for c in range(n_chunk):
            g_copy(d, c).wait_send()
    for d in range(1, W):
        s_copy(d).wait_send()
    for d in range(W):
        ow = lax.rem(w - d + W, W)
        for lm in range(1 if d == 0 else 0, L * M):
            sc_copy(ow, lm).wait_send()


def per_device(acts, grads, projections, lengths, queries, query_ids):
    W, L, M = (lax.axis_size(name) for name in ("wide", "layer", "mp"))
    _, tokens, depth = acts.shape
    rank2 = projections.shape[2]
    rank = rank2 // 2
    ex = lengths.shape[0]
    q_rows = queries.shape[1]
    C = 512
    n_chunk = tokens // C
    mine_pairs = rank // 2 // M
    dma = pltpu.SemaphoreType.DMA
    moves = tokens * depth * 4 + depth * rank2 * 2 + q_rows * depth * 2
    return pl.pallas_call(
        functools.partial(kernel, (W, L, M)),
        out_shape=jax.ShapeDtypeStruct((ex, q_rows * W), F32),
        in_specs=[pl.BlockSpec(memory_space=pl.ANY)] * 6,
        out_specs=pl.BlockSpec(memory_space=pltpu.VMEM),
        scratch_shapes=[
            pltpu.VMEM((n_chunk, C, depth), BF16),
            pltpu.VMEM((n_chunk, C, depth), BF16),
            pltpu.VMEM((depth, rank2), BF16),
            pltpu.VMEM((depth, rank2), BF16),
            pltpu.VMEM((q_rows, depth), BF16),
            pltpu.VMEM((W, 1, q_rows), jnp.int32),
            pltpu.SMEM((ex,), jnp.int32),
            pltpu.VMEM((n_chunk, rank, C), F32),
            pltpu.VMEM((n_chunk, rank, C), BF16),
            pltpu.VMEM((max(M - 1, 1), n_chunk, rank, C), BF16),
            pltpu.VMEM((2, rank * ex, 2 * rank2), F32),
            pltpu.VMEM((rank // 2, ex, rank2), F32),
            pltpu.VMEM((max(M - 1, 1), mine_pairs, ex, rank2), F32),
            pltpu.VMEM((mine_pairs * ex, rank2), BF16),
            pltpu.VMEM((max(W - 1, 1), mine_pairs * ex, rank2), BF16),
            pltpu.VMEM((W, ex, q_rows), F32),
            pltpu.VMEM((W, L * M, ex, q_rows), F32),
            pltpu.VMEM((q_rows * W, q_rows * W), BF16),
            dma((4,)),
            dma((n_chunk,)),
            dma((n_chunk,)),
            dma((max(M - 1, 1), n_chunk)),
            dma((max(M - 1, 1), n_chunk)),
            dma((max(M - 1, 1),)),
            dma((max(M - 1, 1),)),
            dma((max(W - 1, 1),)),
            dma((max(W - 1, 1),)),
            dma((max(W - 1, 1),)),
            dma((max(W - 1, 1),)),
            dma((W * L * M,)),
            dma((W, L * M)),
        ],
        compiler_params=pltpu.CompilerParams(
            collective_id=0, has_side_effects=True, vmem_limit_bytes=56 * 1024 * 1024
        ),
        cost_estimate=pl.CostEstimate(
            flops=tokens * depth * rank2 * 4, bytes_accessed=moves, transcendentals=0
        ),
    )(acts, grads, projections, lengths, queries, query_ids.reshape(1, q_rows))


def solution(mesh):
    return jax.shard_map(
        per_device,
        mesh=mesh,
        in_specs=(
            P("layer", ("groups", "wide"), "mp"),
            P("layer", ("groups", "wide"), "mp"),
            P("layer", "mp", None),
            P(("groups", "wide")),
            P("layer", ("groups", "wide"), "mp"),
            P(("groups", "wide")),
        ),
        out_specs=P(("groups", "wide"), None),
        check_vma=False,
    )
```

```python
import functools

import jax
import jax.numpy as jnp
from jax import lax
from jax.experimental import pallas as pl
from jax.experimental.pallas import tpu as pltpu
from jax.sharding import PartitionSpec as P

MESH = pl.DeviceIdType.MESH
F32 = jnp.float32
BF16 = jnp.bfloat16
NT = (((1,), (1,)), ((), ()))


def each(first, last, body):
    if last - first <= 16:
        for i in range(first, last):
            body(i)
    else:
        pl.loop(first, last)(body)


def kernel(
    sizes, acts, grads, proj, lens, queries, ids, out,
    a_buf, g_buf, w_buf, wx_buf, q_buf, id_buf, len_buf,
    g_own, g_send, g_recv, acc, part, part_recv, s_send, s_recv,
    sc_send, sc_recv, onehot,
    in_sem, a_sem, gr_sem, g_ssem, g_rsem, p_ssem, p_rsem,
    s_ssem, s_rsem, id_ssem, id_rsem, sc_ssem, sc_rsem,
):
    W, L, M = sizes
    N = W * L * M
    w = lax.axis_index("wide")
    l = lax.axis_index("layer")
    m = lax.axis_index("mp")
    me = (w * L + l) * M + m
    n_chunk, C, _ = a_buf.shape
    rank = w_buf.shape[1] // 2
    ex = len_buf.shape[0]
    mine_pairs = part_recv.shape[1]

    def local(src, dst, sem):
        return pltpu.make_async_copy(src, dst, sem)

    def rows(c):
        return pl.ds(pl.multiple_of(c * C, C), C)

    local(proj.at[0], w_buf, in_sem.at[0]).start()
    local(lens, len_buf, in_sem.at[1]).start()
    for c in range(n_chunk):
        local(grads.at[0, rows(c)], g_buf.at[c], gr_sem.at[c]).start()
    for c in range(n_chunk):
        local(acts.at[0, rows(c)], a_buf.at[c], a_sem.at[c]).start()
    local(ids, id_buf.at[w], in_sem.at[2]).start()
    local(queries.at[0], q_buf, in_sem.at[3]).start()

    barrier = pltpu.get_barrier_semaphore()

    def place(d):
        other = lax.rem(me + d, N)
        return other // (L * M), (other // M) % L, other % M

    def greet(d):
        ow, ol, om = place(d)
        pl.semaphore_signal(
            barrier, inc=1, device_id={"wide": ow, "layer": ol, "mp": om}, device_id_type=MESH
        )

    each(1, N, greet)

    sub = lax.broadcasted_iota(jnp.int32, (ex, C), 0)
    lane = lax.broadcasted_iota(jnp.int32, (ex, C), 1)
    local(lens, len_buf, in_sem.at[1]).wait()
    first = jnp.zeros((ex, C), jnp.int32)
    last = jnp.zeros((ex, C), jnp.int32)
    run = jnp.int32(0)
    for e in range(ex):
        first = jnp.where(sub == e, run, first)
        run = run + len_buf[e]
        last = jnp.where(sub == e, run, last)

    local(proj.at[0], w_buf, in_sem.at[0]).wait()
    wx = w_buf[:, :rank]
    wx_buf[...] = jnp.concatenate([wx, wx], axis=1)

    def g_copy(d, c):
        to = lax.rem(m + d, M)
        return pltpu.make_async_remote_copy(
            src_ref=g_send.at[c],
            dst_ref=g_recv.at[d - 1, c],
            send_sem=g_ssem.at[d - 1, c],
            recv_sem=g_rsem.at[d - 1, c],
            device_id={"mp": to},
            device_id_type=MESH,
        )

    def project_g(c):
        local(grads.at[0, rows(c)], g_buf.at[c], gr_sem.at[c]).wait()
        g = jnp.dot(g_buf[c], w_buf[...], preferred_element_type=F32)
        gt = jnp.transpose(g)[rank:, :]
        g_own[c] = gt
        g_send[c] = gt.astype(BF16)

    project_g(0)
    acc[...] = jnp.zeros_like(acc)
    pl.semaphore_wait(barrier, N - 1)
    for d in range(1, M):
        g_copy(d, 0).start()

    @pl.loop(1, n_chunk)
    def _(c):
        project_g(c)
        for d in range(1, M):
            g_copy(d, c).start()

    local(ids, id_buf.at[w], in_sem.at[2]).wait()

    def id_copy(d):
        return pltpu.make_async_remote_copy(
            src_ref=id_buf.at[w],
            dst_ref=id_buf.at[w],
            send_sem=id_ssem.at[d - 1],
            recv_sem=id_rsem.at[d - 1],
            device_id={"wide": lax.rem(w + d, W)},
            device_id_type=MESH,
        )

    for d in range(1, W):
        id_copy(d).start()

    @pl.loop(0, n_chunk)
    def _(c):
        local(acts.at[0, rows(c)], a_buf.at[c], a_sem.at[c]).wait()
        x = jnp.dot(a_buf[c], wx_buf[...], preferred_element_type=F32)
        x_hi = x.astype(BF16)
        x_lo = (x - x_hi.astype(F32)).astype(BF16)
        right = jnp.concatenate([x_hi, x_lo], axis=1)
        g = g_own[c]
        for d in range(1, M):
            g_copy(d, c).wait_recv()
            g = g + g_recv[d - 1, c].astype(F32)
        g_hi = g.astype(BF16).astype(F32)
        g_lo = g - g_hi
        t = lane + c * C
        member = (t >= first) & (t < last)
        for i, side in enumerate((g_hi, g_lo)):
            left = jnp.concatenate(
                [
                    jnp.where(member, jnp.broadcast_to(side[a : a + 1, :], (ex, C)), 0.0)
                    for a in range(rank)
                ],
                axis=0,
            ).astype(BF16)
            acc[i] += jnp.dot(left, right, preferred_element_type=F32)

    wide_lane = lax.broadcasted_iota(jnp.int32, (mine_pairs, ex, 2 * rank), 2)

    def partial(j):
        at = pl.ds(pl.multiple_of(j * (2 * mine_pairs * ex), 2 * mine_pairs * ex), 2 * mine_pairs * ex)
        sums = acc[0, at, : 2 * rank] + acc[0, at, 2 * rank :] + acc[1, at, : 2 * rank]
        sums = sums.reshape(mine_pairs, 2, ex, 2 * rank)
        return jnp.where(wide_lane < rank, sums[:, 0], sums[:, 1])

    def p_copy(d):
        to = lax.rem(m + d, M)
        return pltpu.make_async_remote_copy(
            src_ref=part.at[pl.ds(to * mine_pairs, mine_pairs)],
            dst_ref=part_recv.at[d - 1],
            send_sem=p_ssem.at[d - 1],
            recv_sem=p_rsem.at[d - 1],
            device_id={"mp": to},
            device_id_type=MESH,
        )

    for d in range(1, M):
        to = lax.rem(m + d, M)
        part[pl.ds(to * mine_pairs, mine_pairs)] = partial(to)
        p_copy(d).start()

    root = jnp.zeros((ex, 2 * rank), jnp.int32)
    for e in range(ex):
        root = jnp.where(sub[:, : 2 * rank] == e, len_buf[e], root)
    root = jnp.sqrt(root.astype(F32))

    for d in range(1, W):
        id_copy(d).wait()
    q_rows = id_buf.shape[2]
    for v in range(W):
        number = lax.broadcasted_iota(jnp.int32, (W * q_rows, q_rows), 0)
        onehot[:, v * q_rows : (v + 1) * q_rows] = jnp.where(
            number == id_buf[v], 1.0, 0.0
        ).astype(BF16)
    local(queries.at[0], q_buf, in_sem.at[3]).wait()

    total = partial(m)
    for d in range(1, M):
        p_copy(d).wait_recv()
        total = total + part_recv[d - 1]
    sketch = total / root[None]
    s_send[...] = sketch.reshape(mine_pairs * ex, 2 * rank).astype(BF16)

    def s_copy(d):
        return pltpu.make_async_remote_copy(
            src_ref=s_send,
            dst_ref=s_recv.at[d - 1],
            send_sem=s_ssem.at[d - 1],
            recv_sem=s_rsem.at[d - 1],
            device_id={"wide": lax.rem(w + d, W)},
            device_id_type=MESH,
        )

    for d in range(1, W):
        s_copy(d).start()

    def score(block):
        block = block.astype(F32).reshape(mine_pairs, ex, 2 * rank)
        left = jnp.concatenate([block[k] for k in range(mine_pairs)], axis=1).astype(BF16)
        return lax.dot_general(left, q_buf[...], NT, preferred_element_type=F32)

    def sc_copy(ow, lm):
        other = lax.rem(l * M + m + lm, L * M)
        slot = (lax.rem(ow - w + W, W)) * (L * M) + lm
        return pltpu.make_async_remote_copy(
            src_ref=sc_send.at[ow],
            dst_ref=sc_recv.at[w, lm],
            send_sem=sc_ssem.at[slot],
            recv_sem=sc_rsem.at[w, lm],
            device_id={"wide": ow, "layer": other // M, "mp": other % M},
            device_id_type=MESH,
        )

    own = score(s_send[...])
    sc_send[w] = own
    for lm in range(1, L * M):
        sc_copy(w, lm).start()
    for d in range(1, W):
        s_copy(d).wait_recv()
        ow = lax.rem(w - d + W, W)
        sc_send[ow] = score(s_recv[d - 1])
        for lm in range(L * M):
            sc_copy(ow, lm).start()

    sc_recv[w, 0] = own

    def arrive(v, lm):
        sc = sc_recv.at[v, lm]
        pltpu.make_async_copy(sc, sc, sc_rsem.at[v, lm]).wait()

    for lm in range(1, L * M):
        arrive(w, lm)
    for d in range(1, W):
        v = lax.rem(w + d, W)
        for lm in range(L * M):
            arrive(v, lm)
    blocks = []
    for v in range(W):
        block = sc_recv[v, 0]
        for lm in range(1, L * M):
            block = block + sc_recv[v, lm]
        blocks.append(block)
    scores = jnp.concatenate(blocks, axis=1)
    high = scores.astype(BF16).astype(F32)
    rest = scores - high
    middle = rest.astype(BF16).astype(F32)
    low = rest - middle
    pieces = jnp.concatenate([high, middle, low, jnp.zeros_like(low)], axis=0).astype(BF16)
    placed = lax.dot_general(pieces, onehot[...], NT, preferred_element_type=F32)
    out[...] = placed[:ex] + placed[ex : 2 * ex] + placed[2 * ex : 3 * ex]

    for d in range(1, M):
        p_copy(d).wait_send()
        for c in range(n_chunk):
            g_copy(d, c).wait_send()
    for d in range(1, W):
        s_copy(d).wait_send()
    for d in range(W):
        ow = lax.rem(w - d + W, W)
        for lm in range(1 if d == 0 else 0, L * M):
            sc_copy(ow, lm).wait_send()


def per_device(acts, grads, projections, lengths, queries, query_ids):
    W, L, M = (lax.axis_size(name) for name in ("wide", "layer", "mp"))
    _, tokens, depth = acts.shape
    rank2 = projections.shape[2]
    rank = rank2 // 2
    ex = lengths.shape[0]
    q_rows = queries.shape[1]
    C = 512
    n_chunk = tokens // C
    mine_pairs = rank // 2 // M
    dma = pltpu.SemaphoreType.DMA
    moves = tokens * depth * 4 + depth * rank2 * 2 + q_rows * depth * 2
    return pl.pallas_call(
        functools.partial(kernel, (W, L, M)),
        out_shape=jax.ShapeDtypeStruct((ex, q_rows * W), F32),
        in_specs=[pl.BlockSpec(memory_space=pl.ANY)] * 6,
        out_specs=pl.BlockSpec(memory_space=pltpu.VMEM),
        scratch_shapes=[
            pltpu.VMEM((n_chunk, C, depth), BF16),
            pltpu.VMEM((n_chunk, C, depth), BF16),
            pltpu.VMEM((depth, rank2), BF16),
            pltpu.VMEM((depth, rank2), BF16),
            pltpu.VMEM((q_rows, depth), BF16),
            pltpu.VMEM((W, 1, q_rows), jnp.int32),
            pltpu.SMEM((ex,), jnp.int32),
            pltpu.VMEM((n_chunk, rank, C), F32),
            pltpu.VMEM((n_chunk, rank, C), BF16),
            pltpu.VMEM((max(M - 1, 1), n_chunk, rank, C), BF16),
            pltpu.VMEM((2, rank * ex, 2 * rank2), F32),
            pltpu.VMEM((rank // 2, ex, rank2), F32),
            pltpu.VMEM((max(M - 1, 1), mine_pairs, ex, rank2), F32),
            pltpu.VMEM((mine_pairs * ex, rank2), BF16),
            pltpu.VMEM((max(W - 1, 1), mine_pairs * ex, rank2), BF16),
            pltpu.VMEM((W, ex, q_rows), F32),
            pltpu.VMEM((W, L * M, ex, q_rows), F32),
            pltpu.VMEM((q_rows * W, q_rows * W), BF16),
            dma((4,)),
            dma((n_chunk,)),
            dma((n_chunk,)),
            dma((max(M - 1, 1), n_chunk)),
            dma((max(M - 1, 1), n_chunk)),
            dma((max(M - 1, 1),)),
            dma((max(M - 1, 1),)),
            dma((max(W - 1, 1),)),
            dma((max(W - 1, 1),)),
            dma((max(W - 1, 1),)),
            dma((max(W - 1, 1),)),
            dma((W * L * M,)),
            dma((W, L * M)),
        ],
        compiler_params=pltpu.CompilerParams(
            collective_id=0, has_side_effects=True, vmem_limit_bytes=56 * 1024 * 1024
        ),
        cost_estimate=pl.CostEstimate(
            flops=tokens * depth * rank2 * 4, bytes_accessed=moves, transcendentals=0
        ),
    )(acts, grads, projections, lengths, queries, query_ids.reshape(1, q_rows))


def solution(mesh):
    return jax.shard_map(
        per_device,
        mesh=mesh,
        in_specs=(
            P("layer", ("groups", "wide"), "mp"),
            P("layer", ("groups", "wide"), "mp"),
            P("layer", "mp", None),
            P(("groups", "wide")),
            P("layer", ("groups", "wide"), "mp"),
            P(("groups", "wide")),
        ),
        out_specs=P(("groups", "wide"), None),
        check_vma=False,
    )
```
